32 devices in a mesh: panel: 4 (over z), tx: 2 (over y), ty: 4 (over x, core).
Axes of the slice: x: 2, y: 2, z: 4, core: 2. Of those that a mesh axis runs over, the one named last changes fastest.
Arguments:
- cotangent: float32 [70, 64, 512], P(None, ('panel', 'tx'), 'ty'), may hold values from -30 to 30
- courant: float32 [70, 64, 512], P(None, ('panel', 'tx'), 'ty'), may hold values from 0.1 to 0.9
- faces_first: float32 [70, 64, 512], P(None, ('panel', 'tx'), 'ty'), may hold values from 0.1 to 1
- faces_second: float32 [70, 64, 512], P(None, ('panel', 'tx'), 'ty'), may hold values from 0.1 to 1
- faces_vertical: float32 [69, 64, 512], P(None, ('panel', 'tx'), 'ty'), may hold values from 0.5 to 8
- damping: float32 [70, 64, 512], P(None, ('panel', 'tx'), 'ty'), may hold values from 0.0005 to 0.005
- blocks_fine: float32 [7, 10, 10, 64, 512], P(None, None, None, ('panel', 'tx'), 'ty'), may hold values from 0 to 4
- blocks_half: float32 [7, 10, 10, 32, 256], P(None, None, None, ('panel', 'tx'), 'ty'), may hold values from 0 to 4
- blocks_quarter: float32 [7, 10, 10, 16, 128], P(None, None, None, ('panel', 'tx'), 'ty'), may hold values from 0 to 4
- blocks_eighth: float32 [7, 10, 10, 8, 64], P(None, None, None, ('panel', 'tx'), 'ty'), may hold values from 0 to 4
Outputs:
- solution: float32 [70, 64, 512], P(None, ('panel', 'tx'), 'ty')
- residual: float32 [70, 64, 512], P(None, ('panel', 'tx'), 'ty')
The draws below stay inside these ranges and needn't reach their ends.
All inputs are finite; a program needn't handle non-finite values.
Results may differ from the reference program's by a relative error of at most 0.0003.
Values sent between devices are 32-bit elements; how exact they have to be, the bound alone decides.
A program may use at most 128 MiB of HBM per device.

```python
import jax
import jax.numpy as jnp
from jax import lax

LEV = 70
BLK = 10
GRIDS = 4
ITERS = 3
NA = 64
NB = 512


def loguniform(key, shape, low, high):
    return jnp.exp(jax.random.uniform(key, shape, jnp.float32, jnp.log(low), jnp.log(high)))


def coefficients(key):
    shape = (LEV, NA, NB)
    first = loguniform(jax.random.fold_in(key, 7001), shape, 0.1, 1.0)
    second = loguniform(jax.random.fold_in(key, 7002), shape, 0.1, 1.0)
    vertical = loguniform(jax.random.fold_in(key, 7003), (LEV - 1, NA, NB), 0.5, 8.0)
    damping = loguniform(jax.random.fold_in(key, 7004), shape, 0.0005, 0.005)
    return (first, second, vertical, damping)


def pick_drawn(values, first, second):
    levels, rows, cols = values.shape
    return values.reshape(levels, rows // 2, 2, cols // 2, 2)[:, :, first, :, second]


def restrict_drawn(values):
    levels, rows, cols = values.shape
    return values.reshape(levels, rows // 2, 2, cols // 2, 2).sum(axis=(2, 4))


def coarsen_drawn(weights):
    upper_first, lower_first, upper_second, lower_second, vertical, damping = weights
    return (pick_drawn(upper_first, 1, 0) + pick_drawn(upper_first, 1, 1), pick_drawn(lower_first, 0, 0) + pick_drawn(lower_first, 0, 1), pick_drawn(upper_second, 0, 1) + pick_drawn(upper_second, 1, 1), pick_drawn(lower_second, 0, 0) + pick_drawn(lower_second, 1, 0), restrict_drawn(vertical), restrict_drawn(damping))


def ladder_of(key):
    first, second, vertical, damping = coefficients(key)
    lower_first = jnp.roll(first, 1, axis=1)
    edge = jnp.zeros_like(second[:, :, :1])
    lower_second = jnp.concatenate([edge, second[:, :, :-1]], axis=2)
    ladder = [(first, lower_first, second, lower_second, vertical, damping)]
    for level in range(GRIDS - 1):
        ladder.append(coarsen_drawn(ladder[-1]))
    return ladder


def invert_blocks(weights):
    upper_first, lower_first, upper_second, lower_second, vertical, damping = weights
    levels, rows, cols = damping.shape
    bottom = jnp.zeros_like(vertical[:1])
    column = jnp.concatenate([vertical, bottom], axis=0)
    centre = damping + upper_first + lower_first + upper_second + lower_second
    centre = centre + column + jnp.concatenate([bottom, vertical], axis=0)
    count = levels // BLK
    centre = jnp.moveaxis(centre.reshape(count, BLK, rows, cols), 1, -1)
    couple = jnp.moveaxis(column.reshape(count, BLK, rows, cols), 1, -1)
    identity = jnp.eye(BLK, dtype=jnp.float32)
    above = jnp.eye(BLK, k=1, dtype=jnp.float32)
    below = jnp.eye(BLK, k=-1, dtype=jnp.float32)
    matrix = centre[..., :, None] * identity - couple[..., :, None] * above - couple[..., None, :] * below
    inverse = jnp.linalg.inv(matrix)
    return jnp.transpose(inverse, (0, 3, 4, 1, 2)).astype(jnp.float32)


def draw_cotangent(key, part):
    ramp = 3.0 ** (jnp.arange(NA, dtype=jnp.float32) / NA)
    spread = loguniform(jax.random.fold_in(key, 9002), (NA, NB), 1.0, 10.0)
    scale = ramp[:, None] * spread / 4.0
    values = jnp.clip(jax.random.normal(jax.random.fold_in(key, 9001), (LEV, NA, NB), jnp.float32), -4.0, 4.0)
    return (values * scale[None]).astype(jnp.float32)


def draw_faces_first(key, part):
    return coefficients(key)[0]


def draw_faces_second(key, part):
    return coefficients(key)[1]


def draw_faces_vertical(key, part):
    return coefficients(key)[2]


def draw_damping(key, part):
    return coefficients(key)[3]


def draw_blocks_fine(key, part):
    return invert_blocks(ladder_of(key)[0])


def draw_blocks_half(key, part):
    return invert_blocks(ladder_of(key)[1])


def draw_blocks_quarter(key, part):
    return invert_blocks(ladder_of(key)[2])


def draw_blocks_eighth(key, part):
    return invert_blocks(ladder_of(key)[3])


def block_scale(rng, extent, shards, smallest, largest):
    gain, own = 1.0, jax.random.fold_in(rng, 6)
    for axis_at, blocks in shards:
        heights = jnp.exp(jax.random.uniform(jax.random.fold_in(own, axis_at), (blocks,), jnp.float32, smallest / len(shards), largest / len(shards)))
        gain = gain * jnp.repeat(heights, extent[axis_at] // blocks).reshape([-1 if axis == axis_at else 1 for axis in range(len(extent))])
    return gain


def setup_inputs(seed: int = 0) -> dict:
    keys = jax.random.split(jax.random.key(seed), 11)
    return {
        "cotangent": draw_cotangent(jax.random.fold_in(keys[10], 71), 0),
        "courant": jnp.clip(0.1 + 0.79999997 * jax.random.uniform(keys[1], (LEV, NA, NB), jnp.float32) ** block_scale(keys[1], (LEV, NA, NB), ((1, 8), (2, 4)), -0.2, 0.2), 0.1, 0.9),
        "faces_first": draw_faces_first(jax.random.fold_in(keys[10], 71), 0),
        "faces_second": draw_faces_second(jax.random.fold_in(keys[10], 71), 0),
        "faces_vertical": draw_faces_vertical(jax.random.fold_in(keys[10], 71), 0),
        "damping": draw_damping(jax.random.fold_in(keys[10], 71), 0),
        "blocks_fine": draw_blocks_fine(jax.random.fold_in(keys[10], 71), 0),
        "blocks_half": draw_blocks_half(jax.random.fold_in(keys[10], 71), 0),
        "blocks_quarter": draw_blocks_quarter(jax.random.fold_in(keys[10], 71), 0),
        "blocks_eighth": draw_blocks_eighth(jax.random.fold_in(keys[10], 71), 0),
    }


OMEGA = 0.8

def neighbours(field):
    upper_first = jnp.roll(field, -1, axis=1)
    lower_first = jnp.roll(field, 1, axis=1)
    edge = jnp.zeros_like(field[:, :, :1])
    upper_second = jnp.concatenate([field[:, :, 1:], edge], axis=2)
    lower_second = jnp.concatenate([edge, field[:, :, :-1]], axis=2)
    return (upper_first, lower_first, upper_second, lower_second)

def operate(field, weights):
    upper_first, lower_first, upper_second, lower_second, vertical, damping = weights
    beyond_up, beyond_low, across_up, across_low = neighbours(field)
    total = damping * field + upper_first * (field - beyond_up) + lower_first * (field - beyond_low)
    total = total + upper_second * (field - across_up) + lower_second * (field - across_low)
    flux = vertical * (field[1:] - field[:-1])
    bottom = jnp.zeros_like(field[:1])
    return total - jnp.concatenate([flux, bottom], axis=0) + jnp.concatenate([bottom, flux], axis=0)

def pick(values, first, second):
    levels, rows, cols = values.shape
    return values.reshape(levels, rows // 2, 2, cols // 2, 2)[:, :, first, :, second]

def restrict(values):
    levels, rows, cols = values.shape
    return values.reshape(levels, rows // 2, 2, cols // 2, 2).sum(axis=(2, 4))

def prolong(values):
    return jnp.repeat(jnp.repeat(values, 2, axis=1), 2, axis=2)

def coarsen(weights):
    upper_first, lower_first, upper_second, lower_second, vertical, damping = weights
    return (pick(upper_first, 1, 0) + pick(upper_first, 1, 1), pick(lower_first, 0, 0) + pick(lower_first, 0, 1), pick(upper_second, 0, 1) + pick(upper_second, 1, 1), pick(lower_second, 0, 0) + pick(lower_second, 1, 0), restrict(vertical), restrict(damping))

def block_solve(inverse, field):
    count, width = (inverse.shape[0], inverse.shape[1])
    levels, rows, cols = field.shape
    stacked = field.reshape(count, width, rows, cols)
    product = jnp.einsum('kijab,kjab->kiab', inverse, stacked, precision=lax.Precision.HIGHEST)
    return product.reshape(levels, rows, cols)

def cycle(level, rhs, ladder, blocks):
    weights = ladder[level]
    inverse = blocks[level]
    first = OMEGA * block_solve(inverse, rhs)
    if level == len(blocks) - 1:
        return first + OMEGA * block_solve(inverse, rhs - operate(first, weights))
    remainder = rhs - operate(first, weights)
    coarse = cycle(level + 1, restrict(remainder), ladder, blocks)
    second = first + prolong(coarse)
    return second + OMEGA * block_solve(inverse, rhs - operate(second, weights))

def reference(cotangent, courant, faces_first, faces_second, faces_vertical, damping, blocks_fine, blocks_half, blocks_quarter, blocks_eighth):
    bottom = jnp.zeros_like(cotangent[:1])
    forcing = (1.0 - courant) * cotangent + jnp.concatenate([courant[1:] * cotangent[1:], bottom], axis=0)
    lower_first = jnp.roll(faces_first, 1, axis=1)
    edge = jnp.zeros_like(faces_second[:, :, :1])
    lower_second = jnp.concatenate([edge, faces_second[:, :, :-1]], axis=2)
    weights = (faces_first, lower_first, faces_second, lower_second, faces_vertical, damping)
    ladder = [weights]
    for level in range(GRIDS - 1):
        ladder.append(coarsen(ladder[-1]))
    blocks = (blocks_fine, blocks_half, blocks_quarter, blocks_eighth)
    solution = jnp.zeros_like(forcing)
    residual = forcing
    precond = cycle(0, residual, ladder, blocks)
    direction = precond
    gamma = jnp.sum(residual * precond)
    for step in range(ITERS):
        image = operate(direction, weights)
        alpha = gamma / jnp.sum(direction * image)
        solution = solution + alpha * direction
        residual = residual - alpha * image
        if step + 1 < ITERS:
            precond = cycle(0, residual, ladder, blocks)
            fresh = jnp.sum(residual * precond)
            direction = precond + fresh / gamma * direction
            gamma = fresh
    return (solution, residual)
```

```python
import functools

import jax
import jax.numpy as jnp
from jax import lax
from jax.experimental import pallas as pl
from jax.experimental.pallas import tpu as pltpu
from jax.sharding import PartitionSpec as P

GRIDS = 4
ITERS = 3
OMEGA = 0.8
KEEP = 1.0 - OMEGA
MESH = pl.DeviceIdType.MESH
F32 = jnp.float32


def kernel(
    sizes, count, width,
    cot, cour, ff, fs, fv, damp,
    sol, res,
    M, E, UF, LF, US, LS, C, D, DD, R, X, Z, IM, AL, DR,
    SR, SC, RR, RC, XR, XC, WR, WC, AS, AB,
    s_sem, r_sem, as_sem, ar_sem,
):
    npan, ntx, nty = sizes
    rows, cols = cot.shape[1], cot.shape[2]
    tile = (rows, cols)
    levels = count * width
    na = npan * ntx
    devices = na * nty
    a_me = lax.axis_index("panel") * ntx + lax.axis_index("tx")
    b_me = lax.axis_index("ty")
    me = a_me * nty + b_me

    def place(a, b):
        return (a // ntx, a % ntx, b)

    up_dev = place((a_me + 1) % na, b_me)
    dn_dev = place((a_me + na - 1) % na, b_me)
    rt_dev = place(a_me, (b_me + 1) % nty)
    lf_dev = place(a_me, (b_me + nty - 1) % nty)

    def other(d):
        t = (me + d) % devices
        return place(t // nty, t % nty)

    barrier = pltpu.get_barrier_semaphore()

    @pl.loop(1, devices)
    def _(d):
        pl.semaphore_signal(barrier, inc=1, device_id=other(d), device_id_type=MESH)

    row = lax.broadcasted_iota(jnp.int32, tile, 0)
    lane = lax.broadcasted_iota(jnp.int32, tile, 1)
    zero = jnp.zeros(tile, F32)
    has_left = (b_me > 0).astype(F32)
    has_right = (b_me < nty - 1).astype(F32)

    def bc_row(v):
        return jnp.broadcast_to(v, tile)

    def roll(v, by, axis):
        by = by % tile[axis]
        return v if by == 0 else pltpu.roll(v, by, axis)

    def next_first(v, h, s):
        return jnp.where(row >= rows - s, bc_row(h), roll(v, -s, 0))

    def prev_first(v, h, s):
        return jnp.where(row < s, bc_row(h), roll(v, s, 0))

    def next_second(v, h, s):
        return jnp.where(lane >= cols - s, bc_row(h), roll(v, -s, 1))

    def prev_second(v, h, s):
        return jnp.where(lane < s, bc_row(h), roll(v, s, 1))

    def partner(v, s, axis):
        at = row if axis == 0 else lane
        return jnp.where((at & s) != 0, roll(v, s, axis), roll(v, -s, axis))

    def pair_sum(v, s, axis):
        return v + partner(v, s, axis)

    def pick(v, s, axis, odd):
        at = row if axis == 0 else lane
        keep = ((at & s) != 0) == odd
        return jnp.where(keep, v, partner(v, s, axis))

    def loop(body, carry):
        return lax.fori_loop(0, count, body, carry)

    def pack(slot, l, v, acc):
        lo, hi = acc
        SR[slot, 0, pl.ds(l, 1), :] = v[rows - 1:, :]
        SR[slot, 1, pl.ds(l, 1), :] = v[:1, :]
        lo = jnp.where(lane == l, bc_row(v[:, cols - 1:]), lo)
        hi = jnp.where(lane == l, bc_row(v[:, :1]), hi)
        return lo, hi

    def pack_end(slot, acc):
        SC[slot, 0] = acc[0]
        SC[slot, 1] = acc[1]

    def copies(slot):
        out = []
        for way, dev in ((0, up_dev), (1, dn_dev)):
            out.append(pltpu.make_async_remote_copy(
                SR.at[slot, way], RR.at[slot, way],
                s_sem.at[slot, way], r_sem.at[slot, way], device_id=dev, device_id_type=MESH))
        for way, dev in ((0, rt_dev), (1, lf_dev)):
            out.append(pltpu.make_async_remote_copy(
                SC.at[slot, way], RC.at[slot, way],
                s_sem.at[slot, 2 + way], r_sem.at[slot, 2 + way], device_id=dev, device_id_type=MESH))
        return out

    def start(slot):
        for c in copies(slot):
            c.start()

    def finish(slot):
        for c in copies(slot):
            c.wait()
        RC[slot, 0] = RC[slot, 0] * has_left
        RC[slot, 1] = RC[slot, 1] * has_right

    def exchange(slot):
        start(slot)
        finish(slot)

    def turn(v, k):
        return pltpu.roll(v, (cols - k * width) % cols, 1)

    def coupled(g, k, xs, rows_in, cols_lo, cols_hi, full):
        s = 1 << g
        base = k * width
        clo, chi = turn(cols_lo, k), turn(cols_hi, k)
        out = []
        for a in range(width):
            l = base + a
            v = xs[a]
            h = UF[g, l] * next_first(v, rows_in(1, l), s)
            h = h + LF[g, l] * prev_first(v, rows_in(0, l), s)
            h = h + US[g, l] * next_second(v, chi[:, a:a + 1], s)
            h = h + LS[g, l] * prev_second(v, clo[:, a:a + 1], s)
            out.append(h)
        return out

    def solve(g, k, rs):
        base = k * width
        ys = [rs[0]]
        for a in range(1, width):
            ys.append(rs[a] + M[g, base + a] * ys[-1])
        xs = [None] * width
        xs[-1] = E[g, base + width - 1] * ys[-1]
        for a in range(width - 2, -1, -1):
            xs[a] = E[g, base + a] * ys[a] + M[g, base + a + 1] * xs[a + 1]
        return xs

    def recv_rows(slot):
        return lambda way, l: RR[slot, way, pl.ds(l, 1), :]

    def kept_rows(way, l):
        return XR[way, pl.ds(l, 1), :]

    def across(g, k, field, hs):
        base = k * width
        hs[0] = hs[0] + C[g, base] * field[base]
        hs[-1] = hs[-1] + C[g, base + width] * field[base + width + 1]
        return hs

    def edges(k, acc):
        lo, hi = acc
        for a in range(width):
            l = k * width + a
            SR[0, 0, pl.ds(l, 1), :] = ff[l, rows - 1:, :]
            SR[0, 1, pl.ds(l, 1), :] = ff[l, :1, :]
            w = fs[l]
            lo = jnp.where(lane == l, bc_row(w[:, cols - 1:]), lo)
            hi = jnp.where(lane == l, bc_row(w[:, :1]), hi)
        return lo, hi

    pack_end(0, loop(edges, (zero, zero)))
    for slot in range(2):
        for way in range(2):
            SR[slot, way, pl.ds(levels, SR.shape[2] - levels), :] = jnp.zeros(
                (SR.shape[2] - levels, cols), F32)
    pl.semaphore_wait(barrier, devices - 1)
    start(0)

    for g in range(GRIDS):
        C[g, 0] = zero
        C[g, levels] = zero
        X[g, 0] = zero
        X[g, levels + 1] = zero
    Z[0] = zero
    Z[levels + 1] = zero

    @pl.loop(0, levels - 1)
    def _(l):
        C[0, l + 1] = fv[l]
        res[l] = (1.0 - cour[l]) * cot[l] + cour[l + 1] * cot[l + 1]

    last = levels - 1
    res[last] = (1.0 - cour[last]) * cot[last]

    @pl.loop(0, levels)
    def _(l):
        sol[l] = zero
        AL[l] = zero
        DR[l] = zero

    WR[...] = jnp.zeros(WR.shape, F32)
    WC[...] = jnp.zeros(WC.shape, F32)
    finish(0)

    def grid0(k, carry):
        clo = turn(RC[0, 0], k)
        for a in range(width):
            l = k * width + a
            UF[0, l] = ff[l]
            LF[0, l] = prev_first(ff[l], RR[0, 0, pl.ds(l, 1), :], 1)
            US[0, l] = fs[l]
            LS[0, l] = prev_second(fs[l], clo[:, a:a + 1], 1)
            DD[l] = damp[l]
        return carry

    loop(grid0, 0)

    def factor(g):
        def body(k, carry):
            e = None
            for a in range(width):
                l = k * width + a
                d = DD[l] + UF[g, l] + LF[g, l] + US[g, l] + LS[g, l] + C[g, l] + C[g, l + 1]
                if g == 0:
                    D[l] = d
                if a > 0:
                    m = C[g, l] * e
                    M[g, l] = m
                    d = d - C[g, l] * m
                e = 1.0 / d
                E[g, l] = OMEGA * e
            return carry
        loop(body, 0)

    def coarsen(g):
        s = 1 << g
        def body(k, carry):
            for a in range(width):
                l = k * width + a
                UF[g + 1, l] = pick(pair_sum(UF[g, l], s, 1), s, 0, True)
                LF[g + 1, l] = pick(pair_sum(LF[g, l], s, 1), s, 0, False)
                US[g + 1, l] = pick(pair_sum(US[g, l], s, 0), s, 1, True)
                LS[g + 1, l] = pick(pair_sum(LS[g, l], s, 0), s, 1, False)
                C[g + 1, l + 1] = pair_sum(pair_sum(C[g, l + 1], s, 1), s, 0)
                DD[l] = pair_sum(pair_sum(DD[l], s, 1), s, 0)
            return carry
        loop(body, 0)

    factor(0)
    for g in range(GRIDS - 1):
        coarsen(g)
        factor(g + 1)

    def first(g, slot):
        source = res if g == 0 else R.at[g - 1]
        def body(k, acc):
            base = k * width
            xs = solve(g, k, [source[base + a] for a in range(width)])
            for a in range(width):
                X[g, base + a + 1] = xs[a]
                if slot is not None:
                    acc = pack(slot, base + a, xs[a], acc)
            return acc
        acc = loop(body, (zero, zero) if slot is not None else 0)
        if slot is not None:
            pack_end(slot, acc)

    def remainder(g, rows_in, cols_in):
        s = 1 << g
        source = res if g == 0 else R.at[g - 1]
        clo, chi = cols_in(0), cols_in(1)
        def body(k, carry):
            base = k * width
            xs = [X[g, base + a + 1] for a in range(width)]
            hs = across(g, k, X.at[g], coupled(g, k, xs, rows_in, clo, chi, False))
            for a in range(width):
                v = KEEP * source[base + a] + hs[a]
                R[g, base + a] = pair_sum(pair_sum(v, s, 1), s, 0)
            return carry
        loop(body, 0)

    def last_half(g, slot, out_slot):
        source = res if g == 0 else R.at[g - 1]
        clo, chi = RC[slot, 0], RC[slot, 1]
        rows_in = recv_rows(slot)
        def body(k, acc):
            base = k * width
            xs = [X[g, base + a + 1] for a in range(width)]
            hs = across(g, k, X.at[g], coupled(g, k, xs, rows_in, clo, chi, False))
            zs = solve(g, k, [source[base + a] + hs[a] for a in range(width)])
            for a in range(width):
                z = KEEP * xs[a] + zs[a]
                if g > 0:
                    z = X[g - 1, base + a + 1] + z
                    X[g - 1, base + a + 1] = z
                else:
                    Z[base + a + 1] = z
                acc = pack(out_slot, base + a, z, acc)
            return acc
        pack_end(out_slot, loop(body, (zero, zero)))

    def image(slot, out_slot):
        clo, chi = RC[slot, 0], RC[slot, 1]
        rows_in = recv_rows(slot)
        def body(k, acc):
            rz, iz, pk = acc
            base = k * width
            zs = [Z[base + a + 1] for a in range(width)]
            hs = coupled(0, k, zs, rows_in, clo, chi, True)
            ims = []
            for a in range(width):
                l = base + a
                v = D[l] * zs[a] - hs[a]
                v = v - C[0, l] * Z[l] - C[0, l + 1] * Z[l + 2]
                IM[l] = v
                ims.append(v)
                rz = rz + res[l] * zs[a]
                iz = iz + v * zs[a]
            ws = solve(0, k, ims)
            for a in range(width):
                pk = pack(out_slot, base + a, ws[a], pk)
            return rz, iz, pk
        rz, iz, pk = loop(body, (zero, zero, (zero, zero)))
        pack_end(out_slot, pk)
        return rz, iz

    def sum_copy(it, d):
        return pltpu.make_async_remote_copy(
            AS, AB.at[it, me], as_sem.at[d - 1], ar_sem.at[d - 1],
            device_id=other(d), device_id_type=MESH)

    first(0, 1)
    exchange(1)
    XR[...] = RR[1]
    XC[...] = RC[1]

    def iteration(it, carry):
        gamma, alpha = carry
        remainder(0, kept_rows, lambda way: XC[way])
        for g in range(1, GRIDS):
            slot = (g - 1) % 2
            first(g, slot)
            exchange(slot)
            if g < GRIDS - 1:
                remainder(g, recv_rows(slot), lambda way: RC[slot, way])
        for g in range(GRIDS - 1, -1, -1):
            last_half(g, slot, 1 - slot)
            slot = 1 - slot
            exchange(slot)
        rz, iz = image(slot, 1 - slot)
        slot = 1 - slot
        start(slot)
        top = jnp.sum(rz, axis=0, keepdims=True)
        bot = jnp.sum(iz, axis=0, keepdims=True)
        own = jnp.where(row == 0, bc_row(top), jnp.where(row == 1, bc_row(bot), 0.0))
        AS[...] = own
        AB[it, me] = own

        @pl.loop(1, devices)
        def _(d):
            sum_copy(it, d).start()

        finish(slot)

        @pl.loop(1, devices)
        def _(d):
            sum_copy(it, d).wait()

        total = lax.fori_loop(0, devices, lambda d, t: t + AB[it, d], zero)
        total = jnp.sum(total, axis=1, keepdims=True)
        fresh = bc_row(total[:1])
        curv = bc_row(total[1:2])
        ratio = jnp.where(it == 0, 0.0, fresh / gamma)
        alpha = fresh / (curv - ratio * fresh / alpha)

        @pl.loop(0, count)
        def _(k):
            for a in range(width):
                l = k * width + a
                d = Z[l + 1] + ratio * DR[l]
                DR[l] = d
                sol[l] = sol[l] + alpha * d
                w = IM[l] + ratio * AL[l]
                AL[l] = w
                res[l] = res[l] - alpha * w

        @pl.when(it < ITERS - 1)
        def _():
            for way in range(2):
                w = RC[slot, way] + ratio * WC[way]
                WC[way] = w
                XC[way] = XC[way] - alpha * w
                for t in range(SR.shape[2] // rows):
                    at = pl.ds(t * rows, rows)
                    w = RR[slot, way, at, :] + ratio * WR[way, at, :]
                    WR[way, at, :] = w
                    XR[way, at, :] = XR[way, at, :] - alpha * w
            first(0, None)

        return fresh, alpha

    one = jnp.ones(tile, F32)
    lax.fori_loop(0, ITERS, iteration, (one, one))


def per_device(sizes, cotangent, courant, faces_first, faces_second, faces_vertical, damping, fine, *rest):
    levels, rows, cols = cotangent.shape
    count, width = fine.shape[0], fine.shape[1]
    devices = sizes[0] * sizes[1] * sizes[2]
    padded = -(-levels // rows) * rows
    if levels > cols or rows != 1 << (GRIDS - 1):
        raise ValueError("unsupported tile")
    field = jax.ShapeDtypeStruct((levels, rows, cols), F32)

    def vm(*lead):
        return pltpu.VMEM(lead + (rows, cols), F32)

    vmem = pl.BlockSpec(memory_space=pltpu.VMEM)
    return pl.pallas_call(
        functools.partial(kernel, sizes, count, width),
        out_shape=(field, field),
        in_specs=[vmem] * 6,
        out_specs=(vmem, vmem),
        scratch_shapes=[
            vm(GRIDS, levels), vm(GRIDS, levels),
            vm(GRIDS, levels), vm(GRIDS, levels), vm(GRIDS, levels), vm(GRIDS, levels),
            vm(GRIDS, levels + 1), vm(levels), vm(levels),
            vm(GRIDS - 1, levels), vm(GRIDS, levels + 2), vm(levels + 2),
            vm(levels), vm(levels), vm(levels),
            pltpu.VMEM((2, 2, padded, cols), F32), vm(2, 2),
            pltpu.VMEM((2, 2, padded, cols), F32), vm(2, 2),
            pltpu.VMEM((2, padded, cols), F32), vm(2),
            pltpu.VMEM((2, padded, cols), F32), vm(2),
            vm(), vm(ITERS, devices),
            pltpu.SemaphoreType.DMA((2, 4)), pltpu.SemaphoreType.DMA((2, 4)),
            pltpu.SemaphoreType.DMA((devices - 1,)), pltpu.SemaphoreType.DMA((devices - 1,)),
        ],
        compiler_params=pltpu.CompilerParams(
            collective_id=0, has_side_effects=True, vmem_limit_bytes=48 * 1024 * 1024),
    )(cotangent, courant, faces_first, faces_second, faces_vertical, damping)


def solution(mesh):
    sizes = tuple(mesh.shape[name] for name in ("panel", "tx", "ty"))
    field = P(None, ("panel", "tx"), "ty")
    block = P(None, None, None, ("panel", "tx"), "ty")
    return jax.shard_map(
        functools.partial(per_device, sizes),
        mesh=mesh,
        in_specs=(field,) * 6 + (block,) * 4,
        out_specs=(field, field),
        check_vma=False,
    )
```

```python
import functools

import jax
import jax.numpy as jnp
from jax import lax
from jax.experimental import pallas as pl
from jax.experimental.pallas import tpu as pltpu
from jax.sharding import PartitionSpec as P

GRIDS = 4
ITERS = 3
OMEGA = 0.8
KEEP = 1.0 - OMEGA
MESH = pl.DeviceIdType.MESH
F32 = jnp.float32


def kernel(
    sizes, count, width,
    cot, cour, ff, fs, fv, damp,
    sol, res,
    M, E, UF, LF, US, LS, C, D, DD, R, X, Z, IM, AL, DR,
    SR, SC, RR, RC, QC, XR, XC, WR, WC, AS, AB,
    s_sem, r_sem, as_sem, ar_sem,
):
    npan, ntx, nty = sizes
    rows, cols = cot.shape[1], cot.shape[2]
    tile = (rows, cols)
    levels = count * width
    na = npan * ntx
    devices = na * nty
    a_me = lax.axis_index("panel") * ntx + lax.axis_index("tx")
    b_me = lax.axis_index("ty")
    me = a_me * nty + b_me

    def place(a, b):
        return (a // ntx, a % ntx, b)

    up_dev = place((a_me + 1) % na, b_me)
    dn_dev = place((a_me + na - 1) % na, b_me)
    rt_dev = place(a_me, (b_me + 1) % nty)
    lf_dev = place(a_me, (b_me + nty - 1) % nty)

    def other(d):
        t = (me + d) % devices
        return place(t // nty, t % nty)

    barrier = pltpu.get_barrier_semaphore()

    @pl.loop(1, devices)
    def _(d):
        pl.semaphore_signal(barrier, inc=1, device_id=other(d), device_id_type=MESH)

    row = lax.broadcasted_iota(jnp.int32, tile, 0)
    lane = lax.broadcasted_iota(jnp.int32, tile, 1)
    zero = jnp.zeros(tile, F32)
    has_left = (b_me > 0).astype(F32)
    has_right = (b_me < nty - 1).astype(F32)

    def bc_row(v):
        return jnp.broadcast_to(v, tile)

    def roll(v, by, axis):
        by = by % tile[axis]
        return v if by == 0 else pltpu.roll(v, by, axis)

    def next_first(v, h, s):
        return jnp.where(row >= rows - s, bc_row(h), roll(v, -s, 0))

    def prev_first(v, h, s):
        return jnp.where(row < s, bc_row(h), roll(v, s, 0))

    def next_second(v, h, s):
        return jnp.where(lane >= cols - s, h, roll(v, -s, 1))

    def prev_second(v, h, s):
        return jnp.where(lane < s, h, roll(v, s, 1))

    def partner(v, s, axis):
        at = row if axis == 0 else lane
        return jnp.where((at & s) != 0, roll(v, s, axis), roll(v, -s, axis))

    def pair_sum(v, s, axis):
        return v + partner(v, s, axis)

    def pick(v, s, axis, odd):
        at = row if axis == 0 else lane
        keep = ((at & s) != 0) == odd
        return jnp.where(keep, v, partner(v, s, axis))

    def loop(body, carry):
        for k in range(count):
            carry = body(k, carry)
        return carry

    def tiling(g):
        per = cols // (2 << g)
        return per, -(-levels // per)

    def pack_cols(slot, g, l, v, acc):
        s = 1 << g
        per, _ = tiling(g)
        t, m = l // per, l % per
        moved = roll(v, 2 * s * m + s, 1)
        if m == 0:
            acc = jnp.where(lane < 2 * s, moved, 0.0)
        else:
            acc = jnp.where((lane >= 2 * s * m) & (lane < 2 * s * (m + 1)), moved, acc)
        if m == per - 1 or l == levels - 1:
            SC[slot, t] = acc
        return acc

    def pack(slot, g, l, v, acc):
        SR[slot, 0, pl.ds(l, 1), :] = v[rows - 1:, :]
        SR[slot, 1, pl.ds(l, 1), :] = v[:1, :]
        return pack_cols(slot, g, l, v, acc)

    def copies(slot, g):
        out = []
        for way, dev in ((0, up_dev), (1, dn_dev)):
            out.append(pltpu.make_async_remote_copy(
                SR.at[slot, way], RR.at[slot, way],
                s_sem.at[slot, way], r_sem.at[slot, way], device_id=dev, device_id_type=MESH))
        some = pl.ds(0, tiling(g)[1])
        for way, dev in ((0, rt_dev), (1, lf_dev)):
            out.append(pltpu.make_async_remote_copy(
                SC.at[slot, some], RC.at[slot, way, some],
                s_sem.at[slot, 2 + way], r_sem.at[slot, 2 + way], device_id=dev, device_id_type=MESH))
        return out

    def start(slot, g):
        for c in copies(slot, g):
            c.start()

    def finish(slot, g):
        for c in copies(slot, g):
            c.wait()
        s = 1 << g
        for t in range(tiling(g)[1]):
            low = RC[slot, 0, t] * has_left
            high = RC[slot, 1, t] * has_right
            QC[t] = jnp.where((lane & s) != 0, roll(high, -2 * s, 1), low)

    def exchange(slot, g):
        start(slot, g)
        finish(slot, g)

    def beside(source, g, l):
        per, _ = tiling(g)
        return roll(source[l // per], -(2 << g) * (l % per), 1)

    def coupled(g, k, xs, rows_in, cols_in):
        s = 1 << g
        base = k * width
        out = []
        for a in range(width):
            l = base + a
            v = xs[a]
            q = beside(cols_in, g, l)
            h = UF[g, l] * next_first(v, rows_in(1, l), s)
            h = h + LF[g, l] * prev_first(v, rows_in(0, l), s)
            h = h + US[g, l] * next_second(v, q, s)
            h = h + LS[g, l] * prev_second(v, q, s)
            out.append(h)
        return out

    def solve(g, k, rs):
        base = k * width
        ys = [rs[0]]
        for a in range(1, width):
            ys.append(rs[a] + M[g, base + a] * ys[-1])
        xs = [None] * width
        xs[-1] = E[g, base + width - 1] * ys[-1]
        for a in range(width - 2, -1, -1):
            xs[a] = E[g, base + a] * ys[a] + M[g, base + a + 1] * xs[a + 1]
        return xs

    def recv_rows(slot):
        return lambda way, l: RR[slot, way, pl.ds(l, 1), :]

    def kept_rows(way, l):
        return XR[way, pl.ds(l, 1), :]

    def across(g, k, field, hs):
        base = k * width
        hs[0] = hs[0] + C[g, base] * field[base]
        hs[-1] = hs[-1] + C[g, base + width] * field[base + width + 1]
        return hs

    def edges(k, acc):
        for a in range(width):
            l = k * width + a
            SR[0, 0, pl.ds(l, 1), :] = ff[l, rows - 1:, :]
            SR[0, 1, pl.ds(l, 1), :] = ff[l, :1, :]
            acc = pack_cols(0, 0, l, fs[l], acc)
        return acc

    loop(edges, zero)
    for slot in range(2):
        for way in range(2):
            SR[slot, way, pl.ds(levels, SR.shape[2] - levels), :] = jnp.zeros(
                (SR.shape[2] - levels, cols), F32)
    pl.semaphore_wait(barrier, devices - 1)
    start(0, 0)

    for g in range(GRIDS):
        C[g, 0] = zero
        C[g, levels] = zero
        X[g, 0] = zero
        X[g, levels + 1] = zero
    Z[0] = zero
    Z[levels + 1] = zero

    @pl.loop(0, levels - 1)
    def _(l):
        C[0, l + 1] = fv[l]
        res[l] = (1.0 - cour[l]) * cot[l] + cour[l + 1] * cot[l + 1]

    last = levels - 1
    res[last] = (1.0 - cour[last]) * cot[last]

    @pl.loop(0, levels)
    def _(l):
        sol[l] = zero
        AL[l] = zero
        DR[l] = zero

    WR[...] = jnp.zeros(WR.shape, F32)
    WC[...] = jnp.zeros(WC.shape, F32)
    finish(0, 0)

    def grid0(k, carry):
        for a in range(width):
            l = k * width + a
            UF[0, l] = ff[l]
            LF[0, l] = prev_first(ff[l], RR[0, 0, pl.ds(l, 1), :], 1)
            US[0, l] = fs[l]
            LS[0, l] = prev_second(fs[l], beside(QC, 0, l), 1)
            DD[l] = damp[l]
        return carry

    loop(grid0, 0)

    def factor(g):
        def body(k, carry):
            e = None
            for a in range(width):
                l = k * width + a
                d = DD[l] + UF[g, l] + LF[g, l] + US[g, l] + LS[g, l] + C[g, l] + C[g, l + 1]
                if g == 0:
                    D[l] = d
                if a > 0:
                    m = C[g, l] * e
                    M[g, l] = m
                    d = d - C[g, l] * m
                e = 1.0 / d
                E[g, l] = OMEGA * e
            return carry
        loop(body, 0)

    def coarsen(g):
        s = 1 << g
        def body(k, carry):
            for a in range(width):
                l = k * width + a
                UF[g + 1, l] = pick(pair_sum(UF[g, l], s, 1), s, 0, True)
                LF[g + 1, l] = pick(pair_sum(LF[g, l], s, 1), s, 0, False)
                US[g + 1, l] = pick(pair_sum(US[g, l], s, 0), s, 1, True)
                LS[g + 1, l] = pick(pair_sum(LS[g, l], s, 0), s, 1, False)
                C[g + 1, l + 1] = pair_sum(pair_sum(C[g, l + 1], s, 1), s, 0)
                DD[l] = pair_sum(pair_sum(DD[l], s, 1), s, 0)
            return carry
        loop(body, 0)

    factor(0)
    for g in range(GRIDS - 1):
        coarsen(g)
        factor(g + 1)

    def first(g, slot):
        source = res if g == 0 else R.at[g - 1]
        def body(k, acc):
            base = k * width
            xs = solve(g, k, [source[base + a] for a in range(width)])
            for a in range(width):
                X[g, base + a + 1] = xs[a]
                if slot is not None:
                    acc = pack(slot, g, base + a, xs[a], acc)
            return acc
        loop(body, zero)

    def remainder(g, rows_in, cols_in):
        s = 1 << g
        source = res if g == 0 else R.at[g - 1]
        def body(k, carry):
            base = k * width
            xs = [X[g, base + a + 1] for a in range(width)]
            hs = across(g, k, X.at[g], coupled(g, k, xs, rows_in, cols_in))
            for a in range(width):
                v = KEEP * source[base + a] + hs[a]
                R[g, base + a] = pair_sum(pair_sum(v, s, 1), s, 0)
            return carry
        loop(body, 0)

    def last_half(g, slot, out_slot):
        source = res if g == 0 else R.at[g - 1]
        rows_in = recv_rows(slot)
        def body(k, acc):
            base = k * width
            xs = [X[g, base + a + 1] for a in range(width)]
            hs = across(g, k, X.at[g], coupled(g, k, xs, rows_in, QC))
            zs = solve(g, k, [source[base + a] + hs[a] for a in range(width)])
            for a in range(width):
                z = KEEP * xs[a] + zs[a]
                if g > 0:
                    z = X[g - 1, base + a + 1] + z
                    X[g - 1, base + a + 1] = z
                else:
                    Z[base + a + 1] = z
                acc = pack(out_slot, max(g - 1, 0), base + a, z, acc)
            return acc
        loop(body, zero)

    def image(slot, out_slot):
        rows_in = recv_rows(slot)
        def body(k, acc):
            rz, iz, pk = acc
            base = k * width
            zs = [Z[base + a + 1] for a in range(width)]
            hs = coupled(0, k, zs, rows_in, QC)
            ims = []
            for a in range(width):
                l = base + a
                v = D[l] * zs[a] - hs[a]
                v = v - C[0, l] * Z[l] - C[0, l + 1] * Z[l + 2]
                IM[l] = v
                ims.append(v)
                rz = rz + res[l] * zs[a]
                iz = iz + v * zs[a]
            ws = solve(0, k, ims)
            for a in range(width):
                pk = pack(out_slot, 0, base + a, ws[a], pk)
            return rz, iz, pk
        rz, iz, pk = loop(body, (zero, zero, zero))
        return rz, iz

    def sum_copy(it, d):
        return pltpu.make_async_remote_copy(
            AS, AB.at[it, me], as_sem.at[d - 1], ar_sem.at[d - 1],
            device_id=other(d), device_id_type=MESH)

    first(0, 1)
    exchange(1, 0)
    XR[...] = RR[1]
    for t in range(tiling(0)[1]):
        XC[t] = QC[t]

    def iteration(it, carry):
        gamma, alpha = carry
        remainder(0, kept_rows, XC)
        for g in range(1, GRIDS):
            slot = (g - 1) % 2
            first(g, slot)
            exchange(slot, g)
            if g < GRIDS - 1:
                remainder(g, recv_rows(slot), QC)
        for g in range(GRIDS - 1, -1, -1):
            last_half(g, slot, 1 - slot)
            slot = 1 - slot
            exchange(slot, max(g - 1, 0))
        rz, iz = image(slot, 1 - slot)
        slot = 1 - slot
        start(slot, 0)
        top = jnp.sum(rz, axis=0, keepdims=True)
        bot = jnp.sum(iz, axis=0, keepdims=True)
        own = jnp.where(row == 0, bc_row(top), jnp.where(row == 1, bc_row(bot), 0.0))
        AS[...] = own
        AB[it, me] = own

        @pl.loop(1, devices)
        def _(d):
            sum_copy(it, d).start()

        finish(slot, 0)

        @pl.loop(1, devices)
        def _(d):
            sum_copy(it, d).wait()

        total = lax.fori_loop(0, devices, lambda d, t: t + AB[it, d], zero)
        total = jnp.sum(total, axis=1, keepdims=True)
        fresh = bc_row(total[:1])
        curv = bc_row(total[1:2])
        ratio = jnp.where(it == 0, 0.0, fresh / gamma)
        alpha = fresh / (curv - ratio * fresh / alpha)

        @pl.loop(0, count)
        def _(k):
            for a in range(width):
                l = k * width + a
                d = Z[l + 1] + ratio * DR[l]
                DR[l] = d
                sol[l] = sol[l] + alpha * d
                w = IM[l] + ratio * AL[l]
                AL[l] = w
                res[l] = res[l] - alpha * w

        @pl.when(it < ITERS - 1)
        def _():
            for t in range(tiling(0)[1]):
                w = QC[t] + ratio * WC[t]
                WC[t] = w
                XC[t] = XC[t] - alpha * w
            for way in range(2):
                for t in range(SR.shape[2] // rows):
                    at = pl.ds(t * rows, rows)
                    w = RR[slot, way, at, :] + ratio * WR[way, at, :]
                    WR[way, at, :] = w
                    XR[way, at, :] = XR[way, at, :] - alpha * w
            first(0, None)

        return fresh, alpha

    one = jnp.ones(tile, F32)
    lax.fori_loop(0, ITERS, iteration, (one, one))


def per_device(sizes, cotangent, courant, faces_first, faces_second, faces_vertical, damping, fine, *rest):
    levels, rows, cols = cotangent.shape
    count, width = fine.shape[0], fine.shape[1]
    devices = sizes[0] * sizes[1] * sizes[2]
    most = -(-levels // (cols >> GRIDS))
    fine_tiles = -(-levels // (cols // 2))
    padded = -(-levels // rows) * rows
    if levels > cols or rows != 1 << (GRIDS - 1):
        raise ValueError("unsupported tile")
    field = jax.ShapeDtypeStruct((levels, rows, cols), F32)

    def vm(*lead):
        return pltpu.VMEM(lead + (rows, cols), F32)

    vmem = pl.BlockSpec(memory_space=pltpu.VMEM)
    return pl.pallas_call(
        functools.partial(kernel, sizes, count, width),
        out_shape=(field, field),
        in_specs=[vmem] * 6,
        out_specs=(vmem, vmem),
        scratch_shapes=[
            vm(GRIDS, levels), vm(GRIDS, levels),
            vm(GRIDS, levels), vm(GRIDS, levels), vm(GRIDS, levels), vm(GRIDS, levels),
            vm(GRIDS, levels + 1), vm(levels), vm(levels),
            vm(GRIDS - 1, levels), vm(GRIDS, levels + 2), vm(levels + 2),
            vm(levels), vm(levels), vm(levels),
            pltpu.VMEM((2, 2, padded, cols), F32), vm(2, most),
            pltpu.VMEM((2, 2, padded, cols), F32), vm(2, 2, most), vm(most),
            pltpu.VMEM((2, padded, cols), F32), vm(fine_tiles),
            pltpu.VMEM((2, padded, cols), F32), vm(fine_tiles),
            vm(), vm(ITERS, devices),
            pltpu.SemaphoreType.DMA((2, 4)), pltpu.SemaphoreType.DMA((2, 4)),
            pltpu.SemaphoreType.DMA((devices - 1,)), pltpu.SemaphoreType.DMA((devices - 1,)),
        ],
        compiler_params=pltpu.CompilerParams(
            collective_id=0, has_side_effects=True, vmem_limit_bytes=48 * 1024 * 1024),
    )(cotangent, courant, faces_first, faces_second, faces_vertical, damping)


def solution(mesh):
    sizes = tuple(mesh.shape[name] for name in ("panel", "tx", "ty"))
    field = P(None, ("panel", "tx"), "ty")
    block = P(None, None, None, ("panel", "tx"), "ty")
    return jax.shard_map(
        functools.partial(per_device, sizes),
        mesh=mesh,
        in_specs=(field,) * 6 + (block,) * 4,
        out_specs=(field, field),
        check_vma=False,
    )
```
